128 devices in a mesh: row: 8 (over y, core), col: 16 (over z, x).
Axes of the slice: x: 4, y: 4, z: 4, core: 2. Of those that a mesh axis runs over, the one named last changes fastest.
Arguments:
- factor: float32 [256, 1536, 1536], P(('row', 'col'))
- coupling: bfloat16 [256, 1536, 512], P(('row', 'col')), may hold values from -0.15625 to 0.15625
- boundary: float32 [256, 512, 512], P(('row', 'col'))
- loads: float32 [32, 16384], P(None, ('row', 'col')), may hold values from -6 to 6
- block_ids: int32 [256, 16], P(('row', 'col')), may hold values from 0 to 511, as said below
- live_counts: int32 [256], P(('row', 'col')), may hold values from 8 to 16
Outputs:
- response: float32 [32, 16384], P(None, ('row', 'col'))
The draws below stay inside these ranges and needn't reach their ends.
Inputs may be any that keep to these rules, and one draw needn't show every extreme that they name: `block_ids`: district d lies on device d // 2 (rows then columns of the mesh); its slot s names a block owned by the device in the same mesh row and in mesh column s % 16, where device p owns blocks p * 4 to p * 4 + 3.
All inputs are finite; a program needn't handle non-finite values.
Results may differ from the reference program's by a relative error of at most 0.0003.
Values sent between devices are 32-bit elements; how exact they have to be, the bound alone decides.
No kernel may reach another device: no remote copies, remote signals or barrier semaphores. Data moves between devices by JAX's collectives and lax.ppermute only.
A program may use at most 128 MiB of HBM per device.

```python
import jax
import jax.numpy as jnp
from jax import lax

NI = 1536
BS = 32
NBD = 16
NRHS = 32
DIST_DEV = 2
BLK_DEV = 4
NB = 512
DIST = 256
NBLK = 512
G = 16384
N_COL = 16


def draw_factor(key, part):
    key_lower, key_diag = jax.random.split(jax.random.fold_in(key, 11))
    row_index = lax.broadcasted_iota(jnp.int32, (1, NI, NI), 1)
    col_index = lax.broadcasted_iota(jnp.int32, (1, NI, NI), 2)
    lower_part = jax.random.normal(key_lower, (DIST, NI, NI), jnp.float32) * (0.5 / NI ** 0.5)
    diagonal_part = jax.random.uniform(key_diag, (DIST, NI, 1), jnp.float32, 1.0, 2.0)
    return jnp.where(row_index > col_index, lower_part, jnp.where(row_index == col_index, diagonal_part, 0.0))


def draw_boundary(key, part):
    key_sym, key_diag = jax.random.split(jax.random.fold_in(key, 23))
    noise = jax.random.normal(key_sym, (DIST, NB, NB), jnp.float32) * (0.5 / NB ** 0.5)
    symmetric = noise + jnp.transpose(noise, (0, 2, 1))
    diagonal_part = jax.random.uniform(key_diag, (DIST, NB, 1), jnp.float32, 1.0, 3.0)
    row_index = lax.broadcasted_iota(jnp.int32, (1, NB, NB), 1)
    col_index = lax.broadcasted_iota(jnp.int32, (1, NB, NB), 2)
    return symmetric + jnp.where(row_index == col_index, diagonal_part, 0.0)


def draw_block_ids(key, part):
    district = lax.broadcasted_iota(jnp.int32, (DIST, NBD), 0)
    slot = lax.broadcasted_iota(jnp.int32, (DIST, NBD), 1)
    device = district // DIST_DEV
    mesh_row = device // N_COL
    owner = mesh_row * N_COL + slot % N_COL
    within = jax.random.randint(jax.random.fold_in(key, 37), (DIST, NBD), 0, BLK_DEV, jnp.int32)
    within = jnp.where(district == DIST - 1, BLK_DEV - 1, within)
    within = jnp.where(district == 0, 0, within)
    return owner * BLK_DEV + within


def draw_live_counts(key, part):
    counts = jax.random.randint(jax.random.fold_in(key, 41), (DIST,), NBD // 2, NBD + 1, jnp.int32)
    counts = counts.at[0].set(NBD)
    return counts.at[1].set(NBD // 2)


def steps_of(key, dims, shards, low, high):
    loudness = 1.0
    for axis_at, blocks in shards:
        heights = jax.random.uniform(jax.random.fold_in(jax.random.fold_in(key, 6), axis_at), (blocks,), jnp.float32, low / len(shards), high / len(shards))
        loudness = loudness * jnp.repeat(jnp.exp(heights), dims[axis_at] // blocks).reshape((-1,) + (1,) * (len(dims) - 1 - axis_at))
    return loudness


def bell_draw(own_key, extent, deviation, reach, pieces=(), held_as=jnp.bfloat16):
    loudness = steps_of(own_key, extent, pieces, -0.22, 0.18) if pieces else 1.0
    array = jax.random.normal(own_key, extent, jnp.float32) * deviation * loudness
    return jnp.minimum(jnp.maximum(array, -reach), reach).astype(held_as)


def setup_inputs(seed: int = 0) -> dict:
    key_list = jax.random.split(jax.random.key(seed), 7)
    factor = draw_factor(jax.random.fold_in(key_list[6], 71), 0)
    coupling = bell_draw(key_list[1], (DIST, NI, NB), NI ** -0.5, 0.15625, ((0, 128),))
    boundary = draw_boundary(jax.random.fold_in(key_list[6], 71), 0)
    loads = bell_draw(key_list[3], (NRHS, G), 1.0, 6.0, ((1, 128),), jnp.float32)
    block_ids = draw_block_ids(jax.random.fold_in(key_list[6], 71), 0)
    live_counts = draw_live_counts(jax.random.fold_in(key_list[6], 71), 0)
    return dict(factor=factor, coupling=coupling, boundary=boundary, loads=loads, block_ids=block_ids, live_counts=live_counts)


def district_image(factor, coupling, boundary, picked, live_count):
    solved = jax.scipy.linalg.solve_triangular(factor, coupling.astype(jnp.float32), lower=True)
    schur_block = boundary - lax.dot_general(solved.astype(jnp.float32), solved.astype(jnp.float32), (((0,), (0,)), ((), ())), precision=lax.Precision.HIGHEST, preferred_element_type=jnp.float32)
    weights = (jnp.arange(picked.shape[1]) < live_count).astype(jnp.float32)
    masked = (picked * weights[None, :, None]).reshape(picked.shape[0], -1)
    image = lax.dot_general(masked.astype(jnp.float32), schur_block.astype(jnp.float32), (((1,), (1,)), ((), ())), precision=lax.Precision.HIGHEST, preferred_element_type=jnp.float32)
    return image.reshape(picked.shape) * weights[None, :, None]

def reference(factor, coupling, boundary, loads, block_ids, live_counts):
    load_table = loads.reshape(NRHS, NBLK, BS)

    def one_district(items):
        fac, cpl, bnd, ids, live_count = items
        picked = jnp.take(load_table, ids, axis=1)
        return district_image(fac, cpl, bnd, picked, live_count)
    images = lax.map(one_district, (factor, coupling, boundary, block_ids, live_counts))
    stacked = jnp.transpose(images, (0, 2, 1, 3)).reshape(DIST * NBD, NRHS, BS)
    summed = jax.ops.segment_sum(stacked, block_ids.reshape(-1).astype(jnp.int32), num_segments=NBLK)
    return jnp.transpose(summed, (1, 0, 2)).reshape(NRHS, G)
```

```python
import jax
import jax.numpy as jnp
from jax import lax
from jax.experimental import pallas as pl
from jax.experimental.pallas import tpu as pltpu
from jax.sharding import PartitionSpec as P

BS = 32
TILE = 256
HALF = TILE // 2
BASE = 32
LANES = 128
BF = jnp.bfloat16
F32 = jnp.float32


def split(a):
    high = a.astype(BF)
    return high, (a - high.astype(F32)).astype(BF)


def dot(a, b):
    return jnp.dot(a, b, preferred_element_type=F32)


def dot_t(a, b):
    return lax.dot_general(a, b, (((1,), (1,)), ((), ())), preferred_element_type=F32)


def dot3(a, b):
    both = dot(jnp.concatenate([a[0], a[1]], axis=1), jnp.concatenate([b[0], b[0]], axis=0))
    return both + dot(a[0], b[1])


def base_inverse(tile):
    lane = lax.broadcasted_iota(jnp.int32, (BASE, LANES), 1)
    row = lax.broadcasted_iota(jnp.int32, (BASE, LANES), 0)
    group, column = lane // BASE, lane % BASE
    packed = tile[:BASE]
    for b in range(1, LANES // BASE):
        packed = jnp.where(group == b, tile[b * BASE : (b + 1) * BASE], packed)
    diagonal = jnp.sum(jnp.where(row == column, packed, 0.0), axis=0, keepdims=True)
    recip = 1.0 / diagonal
    unit = jnp.where(row > column, packed * recip, 0.0)
    acc = jnp.where(row == column, 1.0, 0.0).astype(F32)
    parts = [acc[8 * g : 8 * g + 8] for g in range(BASE // 8)]
    for j in range(BASE - 1):
        pivot = parts[j // 8][j % 8 : j % 8 + 1]
        for g in range((j + 1) // 8, BASE // 8):
            index = group[:8] * BASE + j
            factor = jnp.take_along_axis(unit[8 * g : 8 * g + 8], index, axis=1)
            parts[g] = parts[g] - factor * pivot
    rows_scale = jnp.take_along_axis(
        jnp.broadcast_to(recip, (BASE, LANES)), group * BASE + row, axis=1
    )
    inverse = jnp.concatenate(parts, axis=0) * rows_scale
    return jnp.concatenate(
        [jnp.where(group == b, inverse, 0.0) for b in range(LANES // BASE)], axis=0
    )


def prepare_kernel(factor_ref, high_ref, low_ref, ihigh_ref, ilow_ref, held, inv, sem):
    districts, size, _ = factor_ref.shape
    steps = size // TILE
    diag, panels = {}, {}
    for d in range(districts):
        for k in range(steps):
            at = (d, pl.ds(k * TILE, TILE), pl.ds(k * TILE, TILE))
            diag[d, k] = pltpu.make_async_copy(factor_ref.at[at], held.at[at], sem.at[0, d, k])
            diag[d, k].start()
    for d in range(districts):
        for k in range(1, steps):
            at = (d, pl.ds(k * TILE, TILE), pl.ds(0, k * TILE))
            panels[d, k] = pltpu.make_async_copy(factor_ref.at[at], held.at[at], sem.at[1, d, k])
            panels[d, k].start()

    row = lax.broadcasted_iota(jnp.int32, (LANES, LANES), 0)
    col = lax.broadcasted_iota(jnp.int32, (LANES, LANES), 1)
    tiles = [(d, k, t) for d in range(districts) for k in range(steps) for t in range(2)]

    def tile_at(d, k, t, u):
        return held[d, pl.ds(k * TILE + t * HALF, HALF), pl.ds(k * TILE + u * HALF, HALF)]

    for d, k, t in tiles:
        if t == 0:
            diag[d, k].wait()
        inv[2 * (d * steps + k) + t] = base_inverse(tile_at(d, k, t, t))
    width = BASE
    while width < HALF:
        mask = (
            (row // (2 * width) == col // (2 * width))
            & (row % (2 * width) >= width)
            & (col % (2 * width) < width)
        )
        for d, k, t in tiles:
            at = 2 * (d * steps + k) + t
            x = inv[at]
            pair = split(x)
            off = split(jnp.where(mask, tile_at(d, k, t, t), 0.0))
            inv[at] = x - dot3(pair, split(dot3(off, pair)))
        width *= 2
    for d in range(districts):
        for k in range(steps):
            at = d * steps + k
            top, bottom = split(inv[2 * at]), split(inv[2 * at + 1])
            off = split(tile_at(d, k, 1, 0))
            left = split(-dot3(bottom, split(dot3(off, top))))
            zero = jnp.zeros((HALF, HALF), BF)
            for ref, i in ((ihigh_ref, 0), (ilow_ref, 1)):
                ref[at, :HALF, :HALF] = top[i]
                ref[at, :HALF, HALF:] = zero
                ref[at, HALF:, :HALF] = left[i]
                ref[at, HALF:, HALF:] = bottom[i]
    for d in range(districts):
        for k in range(1, steps):
            panels[d, k].wait()
            cols = k * TILE

            @pl.loop(0, TILE // 32)
            def _(i):
                at = (d, pl.ds(pl.multiple_of(k * TILE + i * 32, 32), 32), slice(0, cols))
                high, low = split(held[at])
                high_ref[at] = high
                low_ref[at] = low


def prepare(factor):
    districts, size, _ = factor.shape
    steps = size // TILE
    halves = jax.ShapeDtypeStruct((districts, size, size), BF)
    blocks = jax.ShapeDtypeStruct((districts * steps, TILE, TILE), BF)
    whole = pl.BlockSpec(memory_space=pltpu.VMEM)
    return pl.pallas_call(
        prepare_kernel,
        out_shape=(halves, halves, blocks, blocks),
        in_specs=[pl.BlockSpec(memory_space=pl.ANY)],
        out_specs=(whole,) * 4,
        scratch_shapes=[
            pltpu.VMEM((districts, size, size), F32),
            pltpu.VMEM((districts * steps * 2, LANES, LANES), F32),
            pltpu.SemaphoreType.DMA((2, districts, steps)),
        ],
        compiler_params=pltpu.CompilerParams(vmem_limit_bytes=24 << 20),
        cost_estimate=pl.CostEstimate(
            flops=20 * 10**9, bytes_accessed=12 << 20, transcendentals=0
        ),
        name="prepare",
    )(factor)


def apply_kernel(
    ids_ref,
    live_ref,
    gathered_ref,
    coupling_ref,
    boundary_ref,
    high_ref,
    low_ref,
    ihigh_ref,
    ilow_ref,
    out_ref,
):
    slots, cases, _ = gathered_ref.shape
    districts, size, faces = coupling_ref.shape
    steps = size // TILE
    per = LANES // BS
    group = lax.broadcasted_iota(jnp.int32, (cases, LANES), 1) // BS

    def stack(a):
        return jnp.concatenate(split(a), axis=0)

    def fold(a):
        return a[:cases] + a[cases:]

    masked, total, rest = [], [], []
    for d in range(districts):
        columns = []
        for tile in range(slots // per):
            acc = jnp.zeros((cases, LANES), F32)
            for g in range(per):
                s = tile * per + g
                within = ids_ref[d, s] % per
                piece = pltpu.roll(gathered_ref[s], ((g + per - within) % per) * BS, 1)
                acc = jnp.where((group == g) & (s < live_ref[d]), piece, acc)
            columns.append(acc)
        x = stack(jnp.concatenate(columns, axis=1))
        masked.append(x)
        right = dot_t(x, coupling_ref[d])
        rest.append([fold(right[:, k * TILE : (k + 1) * TILE]) for k in range(steps)])
        high, low = split(boundary_ref[d])
        total.append(fold(dot_t(x, high) + dot_t(x, low)))
    forward = [[None] * steps for _ in range(districts)]
    for k in range(steps):
        for d in range(districts):
            r = stack(rest[d][k])
            at = d * steps + k
            u = fold(dot_t(r, ihigh_ref[at]) + dot_t(r, ilow_ref[at]))
            forward[d][k] = u
            pair = stack(u)
            for j in range(k + 1, steps):
                block = (d, slice(j * TILE, (j + 1) * TILE), slice(k * TILE, (k + 1) * TILE))
                step = dot_t(pair, high_ref[block]) + dot_t(pair, low_ref[block])
                rest[d][j] = rest[d][j] - fold(step)
    for k in reversed(range(steps)):
        for d in range(districts):
            r = stack(forward[d][k])
            at = d * steps + k
            v = fold(dot(r, ihigh_ref[at]) + dot(r, ilow_ref[at]))
            pair = stack(v)
            for j in reversed(range(k)):
                block = (d, slice(k * TILE, (k + 1) * TILE), slice(j * TILE, (j + 1) * TILE))
                step = dot(pair, high_ref[block]) + dot(pair, low_ref[block])
                forward[d][j] = forward[d][j] - fold(step)
            c = coupling_ref[d, k * TILE : (k + 1) * TILE]
            total[d] = total[d] - fold(dot(pair, c))
    for s in range(slots):
        acc = jnp.zeros((cases, LANES), F32)
        for d in range(districts):
            tile, g = s // per, s % per
            within = ids_ref[d, s] % per
            piece = pltpu.roll(
                total[d][:, tile * LANES : (tile + 1) * LANES],
                ((within + per - g) % per) * BS,
                1,
            )
            acc = acc + jnp.where((group == within) & (s < live_ref[d]), piece, 0.0)
        out_ref[s] = acc


def apply(ids, live, gathered, coupling, boundary, prepared):
    scalar = pl.BlockSpec(memory_space=pltpu.SMEM)
    whole = pl.BlockSpec(memory_space=pltpu.VMEM)
    return pl.pallas_call(
        apply_kernel,
        out_shape=jax.ShapeDtypeStruct(gathered.shape, F32),
        in_specs=[scalar, scalar] + [whole] * 7,
        out_specs=whole,
        compiler_params=pltpu.CompilerParams(vmem_limit_bytes=8 << 20),
        cost_estimate=pl.CostEstimate(
            flops=10 * 10**9, bytes_accessed=24 << 20, transcendentals=0
        ),
        name="apply",
    )(ids, live, gathered, coupling, boundary, *prepared)


def body(factor, coupling, boundary, loads, block_ids, live_counts):
    cols = lax.axis_size("col")
    send = jnp.broadcast_to(loads[None], (cols,) + loads.shape)
    gathered = lax.all_to_all(send, "col", 0, 0)
    prepared = prepare(factor)
    back = apply(block_ids, live_counts, gathered, coupling, boundary, prepared)
    return jnp.sum(lax.all_to_all(back, "col", 0, 0), axis=0)


def solution(mesh):
    placed = (
        P(("row", "col"), None, None),
        P(("row", "col"), None, None),
        P(("row", "col"), None, None),
        P(None, ("row", "col")),
        P(("row", "col"), None),
        P(("row", "col")),
    )
    return jax.shard_map(
        body, mesh=mesh, in_specs=placed, out_specs=P(None, ("row", "col")), check_vma=False
    )
```

```python
import jax
import jax.numpy as jnp
from jax import lax
from jax.experimental import pallas as pl
from jax.experimental.pallas import tpu as pltpu
from jax.sharding import PartitionSpec as P

BS = 32
TILE = 256
HALF = TILE // 2
BASE = 16
BATCH = 8
LANES = 128
BF = jnp.bfloat16
F32 = jnp.float32


def split(a):
    high = a.astype(BF)
    return high, (a - high.astype(F32)).astype(BF)


def dot(a, b):
    return jnp.dot(a, b, preferred_element_type=F32)


def dot_t(a, b):
    return lax.dot_general(a, b, (((1,), (1,)), ((), ())), preferred_element_type=F32)


def dot3(a, b):
    both = dot(jnp.concatenate([a[0], a[1]], axis=1), jnp.concatenate([b[0], b[0]], axis=0))
    return both + dot(a[0], b[1])


def base_inverses(tiles):
    lane = lax.broadcasted_iota(jnp.int32, (BASE, LANES), 1)
    row = lax.broadcasted_iota(jnp.int32, (BASE, LANES), 0)
    group, column = lane // BASE, lane % BASE
    units, recips, states = [], [], []
    for tile in tiles:
        packed = tile[:BASE]
        for b in range(1, LANES // BASE):
            packed = jnp.where(group == b, tile[b * BASE : (b + 1) * BASE], packed)
        diagonal = jnp.sum(jnp.where(row == column, packed, 0.0), axis=0, keepdims=True)
        recip = 1.0 / diagonal
        recips.append(recip)
        units.append(jnp.where(row > column, packed * recip, 0.0))
        acc = jnp.where(row == column, 1.0, 0.0).astype(F32)
        states.append([acc[8 * g : 8 * g + 8] for g in range(BASE // 8)])
    for j in range(BASE - 1):
        index = group[:8] * BASE + j
        for unit, parts in zip(units, states):
            pivot = parts[j // 8][j % 8 : j % 8 + 1]
            for g in range((j + 1) // 8, BASE // 8):
                factor = jnp.take_along_axis(unit[8 * g : 8 * g + 8], index, axis=1)
                parts[g] = parts[g] - factor * pivot
    results = []
    for recip, parts in zip(recips, states):
        scale = jnp.take_along_axis(
            jnp.broadcast_to(recip, (BASE, LANES)), group * BASE + row, axis=1
        )
        inverse = jnp.concatenate(parts, axis=0) * scale
        results.append(
            jnp.concatenate(
                [jnp.where(group == b, inverse, 0.0) for b in range(LANES // BASE)], axis=0
            )
        )
    return results


def prepare_kernel(factor_ref, inverse_ref, held, inv, inverse, sem, out_sem):
    districts, size, _ = factor_ref.shape
    steps = size // TILE
    blocks = [(d, k) for k in range(steps) for d in range(districts)]
    loads, stores = {}, []
    for d, k in blocks:
        at = (d, pl.ds(k * TILE, TILE), pl.ds(k * TILE, TILE))
        loads[d, k] = pltpu.make_async_copy(
            factor_ref.at[at], held.at[d * steps + k], sem.at[d * steps + k]
        )
        loads[d, k].start()
    row = lax.broadcasted_iota(jnp.int32, (LANES, LANES), 0)
    col = lax.broadcasted_iota(jnp.int32, (LANES, LANES), 1)
    tiles = [(d * steps + k, t) for d, k in blocks for t in range(2)]

    def tile_at(at, t, u):
        return held[at, pl.ds(t * HALF, HALF), pl.ds(u * HALF, HALF)]

    for first in range(0, len(tiles), BATCH):
        batch = tiles[first : first + BATCH]
        for at, t in batch:
            if t == 0:
                loads[at // steps, at % steps].wait()
        for (at, t), x in zip(batch, base_inverses([tile_at(at, t, t) for at, t in batch])):
            inv[2 * at + t] = x
    width = BASE
    while width < HALF:
        mask = (
            (row // (2 * width) == col // (2 * width))
            & (row % (2 * width) >= width)
            & (col % (2 * width) < width)
        )
        for at, t in tiles:
            x = inv[2 * at + t]
            pair = split(x)
            off = split(jnp.where(mask, tile_at(at, t, t), 0.0))
            inv[2 * at + t] = x - dot3(pair, split(dot3(off, pair)))
        width *= 2
    for d, k in blocks:
        at = d * steps + k
        top, bottom = split(inv[2 * at]), split(inv[2 * at + 1])
        off = split(tile_at(at, 1, 0))
        left = split(-dot3(bottom, split(dot3(off, top))))
        zero = jnp.zeros((HALF, HALF), BF)
        for i in range(2):
            inverse[at, i, :HALF, :HALF] = top[i]
            inverse[at, i, :HALF, HALF:] = zero
            inverse[at, i, HALF:, :HALF] = left[i]
            inverse[at, i, HALF:, HALF:] = bottom[i]
        stores.append(pltpu.make_async_copy(inverse.at[at], inverse_ref.at[at], out_sem.at[at]))
        stores[-1].start()
    for copy in stores:
        copy.wait()


def prepare(factor):
    districts, size, _ = factor.shape
    count = districts * (size // TILE)
    blocks = (count, 2, TILE, TILE)
    anywhere = pl.BlockSpec(memory_space=pltpu.HBM)
    return pl.pallas_call(
        prepare_kernel,
        out_shape=jax.ShapeDtypeStruct(blocks, BF),
        in_specs=[anywhere],
        out_specs=anywhere,
        scratch_shapes=[
            pltpu.VMEM((count, TILE, TILE), F32),
            pltpu.VMEM((count * 2, LANES, LANES), F32),
            pltpu.VMEM(blocks, BF),
            pltpu.SemaphoreType.DMA((count,)),
            pltpu.SemaphoreType.DMA((count,)),
        ],
        compiler_params=pltpu.CompilerParams(vmem_limit_bytes=61 << 20),
        cost_estimate=pl.CostEstimate(
            flops=20 * 10**9, bytes_accessed=12 << 20, transcendentals=0
        ),
        name="prepare",
    )(factor)


def apply_kernel(
    ids_ref,
    live_ref,
    gathered_ref,
    coupling_ref,
    factor_ref,
    boundary_ref,
    inverse_ref,
    out_ref,
    held,
    high,
    low,
    coupling,
    inverse,
    sem,
    inv_sem,
    cpl_sem,
):
    slots, cases, _ = gathered_ref.shape
    districts, size, faces = coupling_ref.shape
    steps = size // TILE
    per = LANES // BS
    group = lax.broadcasted_iota(jnp.int32, (cases, LANES), 1) // BS

    def start(src, dst, at, semaphore):
        copy = pltpu.make_async_copy(src.at[at], dst.at[at], semaphore)
        copy.start()
        return copy

    couplings, inverses, panels = {}, {}, {}
    for d in range(districts):
        couplings[d] = start(coupling_ref, coupling, d, cpl_sem.at[d])
    for k in range(steps):
        for d in range(districts):
            at = d * steps + k
            inverses[d, k] = start(inverse_ref, inverse, at, inv_sem.at[at])
            if k < steps - 1:
                at = (d, pl.ds((k + 1) * TILE, size - (k + 1) * TILE), pl.ds(k * TILE, TILE))
                panels[d, k] = start(factor_ref, held, at, sem.at[d, k])
    def stack(a):
        return jnp.concatenate(split(a), axis=0)

    def fold(a):
        return a[:cases] + a[cases:]

    masked, total, rest = [], [], []
    for d in range(districts):
        columns = []
        for tile in range(slots // per):
            acc = jnp.zeros((cases, LANES), F32)
            for g in range(per):
                s = tile * per + g
                within = ids_ref[d, s] % per
                piece = pltpu.roll(gathered_ref[s], ((g + per - within) % per) * BS, 1)
                acc = jnp.where((group == g) & (s < live_ref[d]), piece, acc)
            columns.append(acc)
        x = stack(jnp.concatenate(columns, axis=1))
        parts = split(boundary_ref[d])
        total.append(fold(dot_t(x, parts[0]) + dot_t(x, parts[1])))
        masked.append(x)
    for d in range(districts):
        couplings[d].wait()
    for d in range(districts):
        right = dot_t(masked[d], coupling[d])
        rest.append([fold(right[:, k * TILE : (k + 1) * TILE]) for k in range(steps)])
    forward = [[None] * steps for _ in range(districts)]
    for k in range(steps):
        if k < 3:
            for copies in (inverses, panels):
                for (d, at), copy in copies.items():
                    if min(at, 2) == k:
                        copy.wait()
        for d in range(districts):
            r = stack(rest[d][k])
            at = d * steps + k
            u = fold(dot_t(r, inverse[at, 0]) + dot_t(r, inverse[at, 1]))
            forward[d][k] = u
            pair = stack(u)
            for j in range(k + 1, steps):
                block = (d, slice(j * TILE, (j + 1) * TILE), slice(k * TILE, (k + 1) * TILE))
                parts = split(held[block])
                high[block], low[block] = parts
                step = dot_t(pair, parts[0]) + dot_t(pair, parts[1])
                rest[d][j] = rest[d][j] - fold(step)
    for k in reversed(range(steps)):
        for d in range(districts):
            r = stack(forward[d][k])
            at = d * steps + k
            v = fold(dot(r, inverse[at, 0]) + dot(r, inverse[at, 1]))
            pair = stack(v)
            for j in reversed(range(k)):
                block = (d, slice(k * TILE, (k + 1) * TILE), slice(j * TILE, (j + 1) * TILE))
                step = dot(pair, high[block]) + dot(pair, low[block])
                forward[d][j] = forward[d][j] - fold(step)
            c = coupling[d, k * TILE : (k + 1) * TILE]
            total[d] = total[d] - fold(dot(pair, c))
    for s in range(slots):
        acc = jnp.zeros((cases, LANES), F32)
        for d in range(districts):
            tile, g = s // per, s % per
            within = ids_ref[d, s] % per
            piece = pltpu.roll(
                total[d][:, tile * LANES : (tile + 1) * LANES],
                ((within + per - g) % per) * BS,
                1,
            )
            acc = acc + jnp.where((group == within) & (s < live_ref[d]), piece, 0.0)
        out_ref[s] = acc


def apply(ids, live, gathered, coupling, factor, boundary, inverse):
    districts, size, faces = coupling.shape
    steps = size // TILE
    scalar = pl.BlockSpec(memory_space=pltpu.SMEM)
    whole = pl.BlockSpec(memory_space=pltpu.VMEM)
    anywhere = pl.BlockSpec(memory_space=pltpu.HBM)
    return pl.pallas_call(
        apply_kernel,
        out_shape=jax.ShapeDtypeStruct(gathered.shape, F32),
        in_specs=[scalar, scalar, whole, anywhere, anywhere, whole, anywhere],
        out_specs=whole,
        scratch_shapes=[
            pltpu.VMEM((districts, size, size - TILE), F32),
            pltpu.VMEM((districts, size, size - TILE), BF),
            pltpu.VMEM((districts, size, size - TILE), BF),
            pltpu.VMEM(coupling.shape, BF),
            pltpu.VMEM(inverse.shape, BF),
            pltpu.SemaphoreType.DMA((districts, steps - 1)),
            pltpu.SemaphoreType.DMA((districts * steps,)),
            pltpu.SemaphoreType.DMA((districts,)),
        ],
        compiler_params=pltpu.CompilerParams(vmem_limit_bytes=50 << 20),
        cost_estimate=pl.CostEstimate(
            flops=10 * 10**9, bytes_accessed=24 << 20, transcendentals=0
        ),
        name="apply",
    )(ids, live, gathered, coupling, factor, boundary, inverse)


def body(factor, coupling, boundary, loads, block_ids, live_counts):
    cols = lax.axis_size("col")
    send = jnp.broadcast_to(loads[None], (cols,) + loads.shape)
    gathered = lax.all_to_all(send, "col", 0, 0)
    back = apply(
        block_ids, live_counts, gathered, coupling, factor, boundary, prepare(factor)
    )
    return jnp.sum(lax.all_to_all(back, "col", 0, 0), axis=0)


def solution(mesh):
    placed = (
        P(("row", "col"), None, None),
        P(("row", "col"), None, None),
        P(("row", "col"), None, None),
        P(None, ("row", "col")),
        P(("row", "col"), None),
        P(("row", "col")),
    )
    return jax.shard_map(
        body, mesh=mesh, in_specs=placed, out_specs=P(None, ("row", "col")), check_vma=False
    )
```

```python
import jax
import jax.numpy as jnp
from jax import lax
from jax.experimental import pallas as pl
from jax.experimental.pallas import tpu as pltpu
from jax.sharding import PartitionSpec as P

BS = 32
TILE = 256
HALF = TILE // 2
BASE = 16
BATCH = 12
LANES = 128
BF = jnp.bfloat16
F32 = jnp.float32


def split(a):
    high = a.astype(BF)
    return high, (a - high.astype(F32)).astype(BF)


def dot(a, b):
    return jnp.dot(a, b, preferred_element_type=F32)


def dot_t(a, b):
    return lax.dot_general(a, b, (((1,), (1,)), ((), ())), preferred_element_type=F32)


def dot3(a, b):
    both = dot(jnp.concatenate([a[0], a[1]], axis=1), jnp.concatenate([b[0], b[0]], axis=0))
    return both + dot(a[0], b[1])


def base_inverses(tiles):
    lane = lax.broadcasted_iota(jnp.int32, (BASE, LANES), 1)
    row = lax.broadcasted_iota(jnp.int32, (BASE, LANES), 0)
    group, column = lane // BASE, lane % BASE
    units, recips, states = [], [], []
    for tile in tiles:
        packed = tile[:BASE]
        for b in range(1, LANES // BASE):
            packed = jnp.where(group == b, tile[b * BASE : (b + 1) * BASE], packed)
        diagonal = jnp.sum(jnp.where(row == column, packed, 0.0), axis=0, keepdims=True)
        recip = 1.0 / diagonal
        recips.append(recip)
        units.append(jnp.where(row > column, packed * recip, 0.0))
        acc = jnp.where(row == column, 1.0, 0.0).astype(F32)
        states.append([acc[8 * g : 8 * g + 8] for g in range(BASE // 8)])
    for j in range(BASE - 1):
        index = group[:8] * BASE + j
        for unit, parts in zip(units, states):
            pivot = parts[j // 8][j % 8 : j % 8 + 1]
            for g in range((j + 1) // 8, BASE // 8):
                factor = jnp.take_along_axis(unit[8 * g : 8 * g + 8], index, axis=1)
                parts[g] = parts[g] - factor * pivot
    results = []
    for recip, parts in zip(recips, states):
        scale = jnp.take_along_axis(
            jnp.broadcast_to(recip, (BASE, LANES)), group * BASE + row, axis=1
        )
        results.append(jnp.concatenate(parts, axis=0) * scale)
    return results


def doubled(tiles, packed, width):
    group = lax.broadcasted_iota(jnp.int32, (width, LANES), 1) // width
    even = group % 2 == 0
    count = LANES // width
    products = []
    for tile, x in zip(tiles, packed):
        below = jnp.where(group == 0, tile[width : 2 * width], 0.0)
        for b in range(2, count, 2):
            below = jnp.where(group == b, tile[(b + 1) * width : (b + 2) * width], below)
        below = jnp.concatenate(split(below), axis=0)
        spread = [
            jnp.where(group == b, half, jnp.zeros_like(half))
            for half in split(x)
            for b in range(count)
        ]
        product = dot(jnp.concatenate([below, below], axis=1), jnp.concatenate(spread, axis=0))
        products.append(product[:width] + product[width:])
    results = []
    for x, product in zip(packed, products):
        odd = jnp.concatenate(split(jnp.where(even, 0.0, x)), axis=0)
        spread = []
        for half in split(product):
            zero = jnp.zeros_like(half)
            for b in range(0, count, 2):
                spread += [zero, jnp.where(group == b, half, zero)]
        product = dot(jnp.concatenate([odd, odd], axis=1), jnp.concatenate(spread, axis=0))
        corner = product[:width] + product[width:]
        results.append(
            jnp.concatenate([jnp.where(even, x, 0.0), jnp.where(even, -corner, x)], axis=0)
        )
    return results


def prepare_kernel(factor_ref, inverse_ref, held, inv, inverse, sem, out_sem):
    districts, size, _ = factor_ref.shape
    steps = size // TILE
    blocks = [(d, k) for k in range(steps) for d in range(districts)]
    loads, stores = {}, []
    for d, k in blocks:
        at = (d, pl.ds(k * TILE, TILE), pl.ds(k * TILE, TILE))
        loads[d, k] = pltpu.make_async_copy(
            factor_ref.at[at], held.at[d * steps + k], sem.at[d * steps + k]
        )
        loads[d, k].start()
    tiles = [(d * steps + k, t) for d, k in blocks for t in range(2)]

    def tile_at(at, t, u):
        return held[at, pl.ds(t * HALF, HALF), pl.ds(u * HALF, HALF)]

    for first in range(0, len(tiles), BATCH):
        batch = tiles[first : first + BATCH]
        for at, t in batch:
            if t == 0:
                loads[at // steps, at % steps].wait()
        diagonal = [tile_at(at, t, t) for at, t in batch]
        packed = base_inverses(diagonal)
        width = BASE
        while width < HALF:
            packed = doubled(diagonal, packed, width)
            width *= 2
        for (at, t), x in zip(batch, packed):
            inv[2 * at + t] = x
    for first in range(0, len(blocks), BATCH // 2):
        group = [d * steps + k for d, k in blocks[first : first + BATCH // 2]]
        pairs = [(split(inv[2 * at]), split(inv[2 * at + 1])) for at in group]
        lefts = [dot3(split(tile_at(at, 1, 0)), top) for at, (top, _) in zip(group, pairs)]
        lefts = [split(-dot3(bottom, split(x))) for x, (_, bottom) in zip(lefts, pairs)]
        zero = jnp.zeros((HALF, HALF), BF)
        for at, (top, bottom), left in zip(group, pairs, lefts):
            for i in range(2):
                inverse[at, i, :HALF, :HALF] = top[i]
                inverse[at, i, :HALF, HALF:] = zero
                inverse[at, i, HALF:, :HALF] = left[i]
                inverse[at, i, HALF:, HALF:] = bottom[i]
            stores.append(
                pltpu.make_async_copy(inverse.at[at], inverse_ref.at[at], out_sem.at[at])
            )
            stores[-1].start()
    for copy in stores:
        copy.wait()


def prepare(factor):
    districts, size, _ = factor.shape
    count = districts * (size // TILE)
    blocks = (count, 2, TILE, TILE)
    anywhere = pl.BlockSpec(memory_space=pltpu.HBM)
    return pl.pallas_call(
        prepare_kernel,
        out_shape=jax.ShapeDtypeStruct(blocks, BF),
        in_specs=[anywhere],
        out_specs=anywhere,
        scratch_shapes=[
            pltpu.VMEM((count, TILE, TILE), F32),
            pltpu.VMEM((count * 2, LANES, LANES), F32),
            pltpu.VMEM(blocks, BF),
            pltpu.SemaphoreType.DMA((count,)),
            pltpu.SemaphoreType.DMA((count,)),
        ],
        compiler_params=pltpu.CompilerParams(vmem_limit_bytes=61 << 20),
        cost_estimate=pl.CostEstimate(
            flops=20 * 10**9, bytes_accessed=12 << 20, transcendentals=0
        ),
        name="prepare",
    )(factor)


def apply_kernel(
    ids_ref,
    live_ref,
    gathered_ref,
    coupling_ref,
    factor_ref,
    boundary_ref,
    inverse_ref,
    out_ref,
    held,
    high,
    low,
    coupling,
    inverse,
    sem,
    inv_sem,
    cpl_sem,
):
    slots, cases, _ = gathered_ref.shape
    districts, size, faces = coupling_ref.shape
    steps = size // TILE
    per = LANES // BS
    group = lax.broadcasted_iota(jnp.int32, (cases, LANES), 1) // BS

    couplings = [
        pltpu.make_async_copy(coupling_ref.at[d], coupling.at[d], cpl_sem.at[d])
        for d in range(districts)
    ]
    stages = []
    for k in range(steps):
        copies = []
        for d in range(districts):
            at = d * steps + k
            copies.append(
                pltpu.make_async_copy(inverse_ref.at[at], inverse.at[at], inv_sem.at[at])
            )
            if k < steps - 1:
                at = (d, pl.ds((k + 1) * TILE, size - (k + 1) * TILE), pl.ds(k * TILE, TILE))
                copies.append(
                    pltpu.make_async_copy(factor_ref.at[at], held.at[at], sem.at[d, k])
                )
        stages.append(copies)
    stages[2] = sum(stages[2:], [])

    def start(copies):
        for copy in copies:
            copy.start()

    def wait(copies):
        for copy in copies:
            copy.wait()

    start(couplings)
    start(stages[0])

    def stack(a):
        return jnp.concatenate(split(a), axis=0)

    def fold(a):
        return a[:cases] + a[cases:]

    masked, total, rest = [], [], []
    for d in range(districts):
        columns = []
        for tile in range(slots // per):
            acc = jnp.zeros((cases, LANES), F32)
            for g in range(per):
                s = tile * per + g
                within = ids_ref[d, s] % per
                piece = pltpu.roll(gathered_ref[s], ((g + per - within) % per) * BS, 1)
                acc = jnp.where((group == g) & (s < live_ref[d]), piece, acc)
            columns.append(acc)
        x = stack(jnp.concatenate(columns, axis=1))
        masked.append(x)
    start(stages[1])
    for d in range(districts):
        parts = split(boundary_ref[d])
        total.append(fold(dot_t(masked[d], parts[0]) + dot_t(masked[d], parts[1])))
    for d in range(districts):
        wait(couplings[d : d + 1])
        if d == 0:
            start(stages[2])
        right = dot_t(masked[d], coupling[d])
        rest.append([fold(right[:, k * TILE : (k + 1) * TILE]) for k in range(steps)])
    everyone = range(districts)
    forward = [[None] * steps for _ in everyone]
    pairs = {}

    def advance(d, k):
        at = d * steps + k
        r = stack(rest[d][k])
        forward[d][k] = fold(dot_t(r, inverse[at, 0]) + dot_t(r, inverse[at, 1]))
        pairs[d, k] = stack(forward[d][k])

    def update(d, k, j):
        block = (d, slice(j * TILE, (j + 1) * TILE), slice(k * TILE, (k + 1) * TILE))
        parts = split(held[block])
        high[block], low[block] = parts
        step = dot_t(pairs[d, k], parts[0]) + dot_t(pairs[d, k], parts[1])
        rest[d][j] = rest[d][j] - fold(step)

    for k in range(steps):
        if k < 3:
            wait(stages[k])
        for d in everyone:
            advance(d, k)
        for d in everyone:
            if d == 1 and k + 1 < steps:
                for e in everyone:
                    update(e, k, k + 1)
            if k > 0:
                for j in range(k + 1, steps):
                    update(d, k - 1, j)

    def retreat(d, k):
        at = d * steps + k
        r = stack(forward[d][k])
        pairs[d, k] = stack(fold(dot(r, inverse[at, 0]) + dot(r, inverse[at, 1])))

    def downdate(d, k, j):
        block = (d, slice(k * TILE, (k + 1) * TILE), slice(j * TILE, (j + 1) * TILE))
        step = dot(pairs[d, k], high[block]) + dot(pairs[d, k], low[block])
        forward[d][j] = forward[d][j] - fold(step)

    def finish(d, k):
        c = coupling[d, k * TILE : (k + 1) * TILE]
        total[d] = total[d] - fold(dot(pairs[d, k], c))

    for k in reversed(range(steps)):
        for d in everyone:
            retreat(d, k)
        for d in everyone:
            if d == 1 and k > 0:
                for e in everyone:
                    downdate(e, k, k - 1)
            if k + 1 < steps:
                finish(d, k + 1)
                for j in reversed(range(k)):
                    downdate(d, k + 1, j)
    for d in everyone:
        finish(d, 0)
    for s in range(slots):
        acc = jnp.zeros((cases, LANES), F32)
        for d in range(districts):
            tile, g = s // per, s % per
            within = ids_ref[d, s] % per
            piece = pltpu.roll(
                total[d][:, tile * LANES : (tile + 1) * LANES],
                ((within + per - g) % per) * BS,
                1,
            )
            acc = acc + jnp.where((group == within) & (s < live_ref[d]), piece, 0.0)
        out_ref[s] = acc


def apply(ids, live, gathered, coupling, factor, boundary, inverse):
    districts, size, faces = coupling.shape
    steps = size // TILE
    scalar = pl.BlockSpec(memory_space=pltpu.SMEM)
    whole = pl.BlockSpec(memory_space=pltpu.VMEM)
    anywhere = pl.BlockSpec(memory_space=pltpu.HBM)
    return pl.pallas_call(
        apply_kernel,
        out_shape=jax.ShapeDtypeStruct(gathered.shape, F32),
        in_specs=[scalar, scalar, whole, anywhere, anywhere, whole, anywhere],
        out_specs=whole,
        scratch_shapes=[
            pltpu.VMEM((districts, size, size - TILE), F32),
            pltpu.VMEM((districts, size, size - TILE), BF),
            pltpu.VMEM((districts, size, size - TILE), BF),
            pltpu.VMEM(coupling.shape, BF),
            pltpu.VMEM(inverse.shape, BF),
            pltpu.SemaphoreType.DMA((districts, steps - 1)),
            pltpu.SemaphoreType.DMA((districts * steps,)),
            pltpu.SemaphoreType.DMA((districts,)),
        ],
        compiler_params=pltpu.CompilerParams(vmem_limit_bytes=50 << 20),
        cost_estimate=pl.CostEstimate(
            flops=10 * 10**9, bytes_accessed=24 << 20, transcendentals=0
        ),
        name="apply",
    )(ids, live, gathered, coupling, factor, boundary, inverse)


def body(factor, coupling, boundary, loads, block_ids, live_counts):
    cols = lax.axis_size("col")
    send = jnp.broadcast_to(loads[None], (cols,) + loads.shape)
    gathered = lax.all_to_all(send, "col", 0, 0)
    back = apply(
        block_ids, live_counts, gathered, coupling, factor, boundary, prepare(factor)
    )
    return jnp.sum(lax.all_to_all(back, "col", 0, 0), axis=0)


def solution(mesh):
    placed = (
        P(("row", "col"), None, None),
        P(("row", "col"), None, None),
        P(("row", "col"), None, None),
        P(None, ("row", "col")),
        P(("row", "col"), None),
        P(("row", "col")),
    )
    return jax.shard_map(
        body, mesh=mesh, in_specs=placed, out_specs=P(None, ("row", "col")), check_vma=False
    )
```

```python
import jax
import jax.numpy as jnp
from jax import lax
from jax.experimental import pallas as pl
from jax.experimental.pallas import tpu as pltpu
from jax.sharding import PartitionSpec as P

BS = 32
TILE = 256
HALF = TILE // 2
BASE = 16
BATCH = 12
LANES = 128
BF = jnp.bfloat16
F32 = jnp.float32


def split(a):
    high = a.astype(BF)
    return high, (a - high.astype(F32)).astype(BF)


def dot(a, b):
    return jnp.dot(a, b, preferred_element_type=F32)


def dot_t(a, b):
    return lax.dot_general(a, b, (((1,), (1,)), ((), ())), preferred_element_type=F32)


def dot3(a, b):
    both = dot(jnp.concatenate([a[0], a[1]], axis=1), jnp.concatenate([b[0], b[0]], axis=0))
    return both + dot(a[0], b[1])


def base_inverses(tiles):
    lane = lax.broadcasted_iota(jnp.int32, (BASE, LANES), 1)
    row = lax.broadcasted_iota(jnp.int32, (BASE, LANES), 0)
    group, column = lane // BASE, lane % BASE
    units, recips, states = [], [], []
    for tile in tiles:
        packed = tile[:BASE]
        for b in range(1, LANES // BASE):
            packed = jnp.where(group == b, tile[b * BASE : (b + 1) * BASE], packed)
        diagonal = jnp.sum(jnp.where(row == column, packed, 0.0), axis=0, keepdims=True)
        recip = 1.0 / diagonal
        recips.append(recip)
        units.append(jnp.where(row > column, packed * recip, 0.0))
        acc = jnp.where(row == column, 1.0, 0.0).astype(F32)
        states.append([acc[8 * g : 8 * g + 8] for g in range(BASE // 8)])
    for j in range(BASE - 1):
        index = group[:8] * BASE + j
        for unit, parts in zip(units, states):
            pivot = parts[j // 8][j % 8 : j % 8 + 1]
            for g in range((j + 1) // 8, BASE // 8):
                factor = jnp.take_along_axis(unit[8 * g : 8 * g + 8], index, axis=1)
                parts[g] = parts[g] - factor * pivot
    results = []
    for recip, parts in zip(recips, states):
        scale = jnp.take_along_axis(
            jnp.broadcast_to(recip, (BASE, LANES)), group * BASE + row, axis=1
        )
        results.append(jnp.concatenate(parts, axis=0) * scale)
    return results


def doubled(tiles, packed, width):
    group = lax.broadcasted_iota(jnp.int32, (width, LANES), 1) // width
    even = group % 2 == 0
    count = LANES // width
    products = []
    for tile, x in zip(tiles, packed):
        below = jnp.where(group == 0, tile[width : 2 * width], 0.0)
        for b in range(2, count, 2):
            below = jnp.where(group == b, tile[(b + 1) * width : (b + 2) * width], below)
        below = jnp.concatenate(split(below), axis=0)
        spread = [
            jnp.where(group == b, half, jnp.zeros_like(half))
            for half in split(x)
            for b in range(count)
        ]
        product = dot(jnp.concatenate([below, below], axis=1), jnp.concatenate(spread, axis=0))
        products.append(product[:width] + product[width:])
    results = []
    for x, product in zip(packed, products):
        odd = jnp.concatenate(split(jnp.where(even, 0.0, x)), axis=0)
        spread = []
        for half in split(product):
            zero = jnp.zeros_like(half)
            for b in range(0, count, 2):
                spread += [zero, jnp.where(group == b, half, zero)]
        product = dot(jnp.concatenate([odd, odd], axis=1), jnp.concatenate(spread, axis=0))
        corner = product[:width] + product[width:]
        results.append(
            jnp.concatenate([jnp.where(even, x, 0.0), jnp.where(even, -corner, x)], axis=0)
        )
    return results


def apply_kernel(
    ids_ref,
    live_ref,
    gathered_ref,
    coupling_ref,
    factor_ref,
    boundary_ref,
    out_ref,
    inv,
    inverse,
    high,
    low,
):
    slots, cases, _ = gathered_ref.shape
    districts, size, faces = coupling_ref.shape
    steps = size // TILE
    per = LANES // BS
    everyone = range(districts)

    blocks = [(d, k) for k in range(steps) for d in everyone]

    def tile_at(d, k, t, u):
        top, left = k * TILE + t * HALF, k * TILE + u * HALF
        return factor_ref[d, pl.ds(top, HALF), pl.ds(left, HALF)]

    for first in range(0, len(blocks), BATCH // 2):
        batch = blocks[first : first + BATCH // 2]
        diagonal = [tile_at(d, k, t, t) for d, k in batch for t in range(2)]
        packed = base_inverses(diagonal)
        width = BASE
        while width < HALF:
            packed = doubled(diagonal, packed, width)
            width *= 2
        pairs = [(split(packed[2 * i]), split(packed[2 * i + 1])) for i in range(len(batch))]
        lefts = [dot3(split(tile_at(*at, 1, 0)), top) for at, (top, _) in zip(batch, pairs)]
        lefts = [split(-dot3(bottom, split(x))) for x, (_, bottom) in zip(lefts, pairs)]
        zero = jnp.zeros((HALF, HALF), BF)
        for (d, k), (top, bottom), left in zip(batch, pairs, lefts):
            at = d * steps + k
            for i in range(2):
                inverse[at, i, :HALF, :HALF] = top[i]
                inverse[at, i, :HALF, HALF:] = zero
                inverse[at, i, HALF:, :HALF] = left[i]
                inverse[at, i, HALF:, HALF:] = bottom[i]

    group = lax.broadcasted_iota(jnp.int32, (cases, LANES), 1) // BS

    def stack(a):
        return jnp.concatenate(split(a), axis=0)

    def fold(a):
        return a[:cases] + a[cases:]

    masked, total, rest = [], [], []
    for d in range(districts):
        columns = []
        for tile in range(slots // per):
            acc = jnp.zeros((cases, LANES), F32)
            for g in range(per):
                s = tile * per + g
                within = ids_ref[d, s] % per
                piece = pltpu.roll(gathered_ref[s], ((g + per - within) % per) * BS, 1)
                acc = jnp.where((group == g) & (s < live_ref[d]), piece, acc)
            columns.append(acc)
        x = stack(jnp.concatenate(columns, axis=1))
        masked.append(x)
    for d in range(districts):
        parts = split(boundary_ref[d])
        total.append(fold(dot_t(masked[d], parts[0]) + dot_t(masked[d], parts[1])))
    for d in range(districts):
        right = dot_t(masked[d], coupling_ref[d])
        rest.append([fold(right[:, k * TILE : (k + 1) * TILE]) for k in range(steps)])
    forward = [[None] * steps for _ in everyone]
    pairs = {}

    def advance(d, k):
        at = d * steps + k
        r = stack(rest[d][k])
        forward[d][k] = fold(dot_t(r, inverse[at, 0]) + dot_t(r, inverse[at, 1]))
        pairs[d, k] = stack(forward[d][k])

    def update(d, k, j):
        block = (d, slice(j * TILE, (j + 1) * TILE), slice(k * TILE, (k + 1) * TILE))
        parts = split(factor_ref[block])
        high[block], low[block] = parts
        step = dot_t(pairs[d, k], parts[0]) + dot_t(pairs[d, k], parts[1])
        rest[d][j] = rest[d][j] - fold(step)

    for k in range(steps):
        for d in everyone:
            advance(d, k)
        for d in everyone:
            if d == 1 and k + 1 < steps:
                for e in everyone:
                    update(e, k, k + 1)
            if k > 0:
                for j in range(k + 1, steps):
                    update(d, k - 1, j)

    def retreat(d, k):
        at = d * steps + k
        r = stack(forward[d][k])
        pairs[d, k] = stack(fold(dot(r, inverse[at, 0]) + dot(r, inverse[at, 1])))

    def downdate(d, k, j):
        block = (d, slice(k * TILE, (k + 1) * TILE), slice(j * TILE, (j + 1) * TILE))
        step = dot(pairs[d, k], high[block]) + dot(pairs[d, k], low[block])
        forward[d][j] = forward[d][j] - fold(step)

    def finish(d, k):
        c = coupling_ref[d, k * TILE : (k + 1) * TILE]
        total[d] = total[d] - fold(dot(pairs[d, k], c))

    for k in reversed(range(steps)):
        for d in everyone:
            retreat(d, k)
        for d in everyone:
            if d == 1 and k > 0:
                for e in everyone:
                    downdate(e, k, k - 1)
            if k + 1 < steps:
                finish(d, k + 1)
                for j in reversed(range(k)):
                    downdate(d, k + 1, j)
    for d in everyone:
        finish(d, 0)
    for s in range(slots):
        acc = jnp.zeros((cases, LANES), F32)
        for d in range(districts):
            tile, g = s // per, s % per
            within = ids_ref[d, s] % per
            piece = pltpu.roll(
                total[d][:, tile * LANES : (tile + 1) * LANES],
                ((within + per - g) % per) * BS,
                1,
            )
            acc = acc + jnp.where((group == within) & (s < live_ref[d]), piece, 0.0)
        out_ref[s] = acc


def apply(ids, live, gathered, coupling, factor, boundary):
    districts, size, faces = coupling.shape
    count = districts * (size // TILE)
    scalar = pl.BlockSpec(memory_space=pltpu.SMEM)
    whole = pl.BlockSpec(memory_space=pltpu.VMEM)
    return pl.pallas_call(
        apply_kernel,
        out_shape=jax.ShapeDtypeStruct(gathered.shape, F32),
        in_specs=[scalar, scalar] + [whole] * 4,
        out_specs=whole,
        scratch_shapes=[
            pltpu.VMEM((count * 2, LANES, LANES), F32),
            pltpu.VMEM((count, 2, TILE, TILE), BF),
            pltpu.VMEM((districts, size, size - TILE), BF),
            pltpu.VMEM((districts, size, size - TILE), BF),
        ],
        compiler_params=pltpu.CompilerParams(vmem_limit_bytes=28 << 20),
        cost_estimate=pl.CostEstimate(
            flops=10 * 10**9, bytes_accessed=24 << 20, transcendentals=0
        ),
        name="apply",
    )(ids, live, gathered, coupling, factor, boundary)


def pack_kernel(loads_ref, out_ref):
    loads = loads_ref[...]
    for p in range(out_ref.shape[0]):
        out_ref[p] = loads


def pack(loads, copies):
    whole = pl.BlockSpec(memory_space=pltpu.VMEM)
    return pl.pallas_call(
        pack_kernel,
        out_shape=jax.ShapeDtypeStruct((copies,) + loads.shape, F32),
        in_specs=[whole],
        out_specs=whole,
        compiler_params=pltpu.CompilerParams(vmem_limit_bytes=2 << 20),
        cost_estimate=pl.CostEstimate(
            flops=30 * 10**9, bytes_accessed=1 << 20, transcendentals=0
        ),
        name="pack",
    )(loads)


def body(factor, coupling, boundary, loads, block_ids, live_counts):
    gathered = lax.all_to_all(pack(loads, lax.axis_size("col")), "col", 0, 0)
    back = apply(block_ids, live_counts, gathered, coupling, factor, boundary)
    return jnp.sum(lax.all_to_all(back, "col", 0, 0), axis=0)


def solution(mesh):
    placed = (
        P(("row", "col"), None, None),
        P(("row", "col"), None, None),
        P(("row", "col"), None, None),
        P(None, ("row", "col")),
        P(("row", "col"), None),
        P(("row", "col")),
    )
    return jax.shard_map(
        body, mesh=mesh, in_specs=placed, out_specs=P(None, ("row", "col")), check_vma=False
    )
```

```python
import jax
import jax.numpy as jnp
from jax import lax
from jax.experimental import pallas as pl
from jax.experimental.pallas import tpu as pltpu
from jax.sharding import PartitionSpec as P

BS = 32
TILE = 256
HALF = TILE // 2
BASE = 16
BATCH = 12
LANES = 128
BF = jnp.bfloat16
F32 = jnp.float32


def split(a):
    high = a.astype(BF)
    return high, (a - high.astype(F32)).astype(BF)


def dot(a, b):
    return jnp.dot(a, b, preferred_element_type=F32)


def dot_t(a, b):
    return lax.dot_general(a, b, (((1,), (1,)), ((), ())), preferred_element_type=F32)


def dot3(a, b):
    both = dot(jnp.concatenate([a[0], a[1]], axis=1), jnp.concatenate([b[0], b[0]], axis=0))
    return both + dot(a[0], b[1])


def base_inverses(tiles):
    lane = lax.broadcasted_iota(jnp.int32, (BASE, LANES), 1)
    row = lax.broadcasted_iota(jnp.int32, (BASE, LANES), 0)
    group, column = lane // BASE, lane % BASE
    units, recips, states = [], [], []
    for tile in tiles:
        packed = tile[:BASE]
        for b in range(1, LANES // BASE):
            packed = jnp.where(group == b, tile[b * BASE : (b + 1) * BASE], packed)
        diagonal = jnp.sum(jnp.where(row == column, packed, 0.0), axis=0, keepdims=True)
        recip = 1.0 / diagonal
        recips.append(recip)
        units.append(jnp.where(row > column, packed * recip, 0.0))
        acc = jnp.where(row == column, 1.0, 0.0).astype(F32)
        states.append([acc[8 * g : 8 * g + 8] for g in range(BASE // 8)])
    for j in range(BASE - 1):
        yield
        index = group[:8] * BASE + j
        for unit, parts in zip(units, states):
            pivot = parts[j // 8][j % 8 : j % 8 + 1]
            for g in range((j + 1) // 8, BASE // 8):
                factor = jnp.take_along_axis(unit[8 * g : 8 * g + 8], index, axis=1)
                parts[g] = parts[g] - factor * pivot
    results = []
    for recip, parts in zip(recips, states):
        scale = jnp.take_along_axis(
            jnp.broadcast_to(recip, (BASE, LANES)), group * BASE + row, axis=1
        )
        results.append(jnp.concatenate(parts, axis=0) * scale)
    return results


def together(*tasks):
    tasks = [list(task) for task in tasks]
    while tasks:
        for task in list(tasks):
            for _ in range(task[1]):
                if next(task[0], tasks) is tasks:
                    tasks.remove(task)
                    break


def doubled(tiles, packed, width):
    group = lax.broadcasted_iota(jnp.int32, (width, LANES), 1) // width
    even = group % 2 == 0
    count = LANES // width
    products = []
    for tile, x in zip(tiles, packed):
        below = jnp.where(group == 0, tile[width : 2 * width], 0.0)
        for b in range(2, count, 2):
            below = jnp.where(group == b, tile[(b + 1) * width : (b + 2) * width], below)
        below = jnp.concatenate(split(below), axis=0)
        spread = [
            jnp.where(group == b, half, jnp.zeros_like(half))
            for half in split(x)
            for b in range(count)
        ]
        product = dot(jnp.concatenate([below, below], axis=1), jnp.concatenate(spread, axis=0))
        products.append(product[:width] + product[width:])
    yield
    results = []
    for x, product in zip(packed, products):
        odd = jnp.concatenate(split(jnp.where(even, 0.0, x)), axis=0)
        spread = []
        for half in split(product):
            zero = jnp.zeros_like(half)
            for b in range(0, count, 2):
                spread += [zero, jnp.where(group == b, half, zero)]
        product = dot(jnp.concatenate([odd, odd], axis=1), jnp.concatenate(spread, axis=0))
        corner = product[:width] + product[width:]
        results.append(
            jnp.concatenate([jnp.where(even, x, 0.0), jnp.where(even, -corner, x)], axis=0)
        )
    return results


def apply_kernel(
    ids_ref,
    live_ref,
    gathered_ref,
    coupling_ref,
    factor_ref,
    boundary_ref,
    out_ref,
    inv,
    inverse,
    high,
    low,
):
    slots, cases, _ = gathered_ref.shape
    districts, size, faces = coupling_ref.shape
    steps = size // TILE
    per = LANES // BS
    everyone = range(districts)

    blocks = [(d, k) for k in range(steps) for d in everyone]

    def tile_at(d, k, t, u):
        top, left = k * TILE + t * HALF, k * TILE + u * HALF
        return factor_ref[d, pl.ds(top, HALF), pl.ds(left, HALF)]

    def invert(batch):
        diagonal = [tile_at(d, k, t, t) for d, k in batch for t in range(2)]
        packed = yield from base_inverses(diagonal)
        width = BASE
        while width < HALF:
            yield
            packed = yield from doubled(diagonal, packed, width)
            width *= 2
        pairs = [(split(packed[2 * i]), split(packed[2 * i + 1])) for i in range(len(batch))]
        yield
        lefts = [dot3(split(tile_at(*at, 1, 0)), top) for at, (top, _) in zip(batch, pairs)]
        yield
        lefts = [split(-dot3(bottom, split(x))) for x, (_, bottom) in zip(lefts, pairs)]
        yield
        zero = jnp.zeros((HALF, HALF), BF)
        for (d, k), (top, bottom), left in zip(batch, pairs, lefts):
            at = d * steps + k
            for i in range(2):
                inverse[at, i, :HALF, :HALF] = top[i]
                inverse[at, i, :HALF, HALF:] = zero
                inverse[at, i, HALF:, :HALF] = left[i]
                inverse[at, i, HALF:, HALF:] = bottom[i]

    group = lax.broadcasted_iota(jnp.int32, (cases, LANES), 1) // BS

    def stack(a):
        return jnp.concatenate(split(a), axis=0)

    def fold(a):
        return a[:cases] + a[cases:]

    masked = []
    total, rest = [[] for _ in everyone], [[] for _ in everyone]
    def gather():
        for d in everyone:
            columns = []
            for tile in range(slots // per):
                acc = jnp.zeros((cases, LANES), F32)
                for g in range(per):
                    s = tile * per + g
                    within = ids_ref[d, s] % per
                    piece = pltpu.roll(gathered_ref[s], ((g + per - within) % per) * BS, 1)
                    acc = jnp.where((group == g) & (s < live_ref[d]), piece, acc)
                columns.append(acc)
            masked.append(stack(jnp.concatenate(columns, axis=1)))
        for k in range(steps):
            for d in everyone:
                yield
                right = dot_t(masked[d], coupling_ref[d, k * TILE : (k + 1) * TILE])
                rest[d].append(fold(right))

    def direct():
        for part in range(faces // LANES):
            for d in everyone:
                yield
                rows = slice(part * LANES, (part + 1) * LANES)
                parts = split(boundary_ref[d, rows])
                image = dot_t(masked[d], parts[0]) + dot_t(masked[d], parts[1])
                total[d].append(fold(image))

    forward = [[None] * steps for _ in everyone]
    pairs = {}

    def advance(d, k):
        at = d * steps + k
        r = stack(rest[d][k])
        forward[d][k] = fold(dot_t(r, inverse[at, 0]) + dot_t(r, inverse[at, 1]))
        pairs[d, k] = stack(forward[d][k])

    def update(d, k, j):
        block = (d, slice(j * TILE, (j + 1) * TILE), slice(k * TILE, (k + 1) * TILE))
        parts = split(factor_ref[block])
        high[block], low[block] = parts
        turned = split(factor_ref[block].T)
        step = dot(pairs[d, k], turned[0]) + dot(pairs[d, k], turned[1])
        rest[d][j] = rest[d][j] - fold(step)

    def solve(first, last):
        for k in range(first, last):
            for d in everyone:
                advance(d, k)
                yield
            for d in everyone:
                if d == 1 and k + 1 < steps:
                    for e in everyone:
                        update(e, k, k + 1)
                        yield
                if k > 0:
                    for j in range(k + 1, steps):
                        update(d, k - 1, j)
                        yield

    half = len(blocks) // 3
    together((invert(blocks[:half]), 1), (gather(), 1))
    together((invert(blocks[half:]), 1), (solve(0, 2), 1))
    together((solve(2, steps), 1), (direct(), 1))
    total = [jnp.concatenate(halves, axis=1) for halves in total]

    def retreat(d, k):
        at = d * steps + k
        r = stack(forward[d][k])
        pairs[d, k] = stack(fold(dot(r, inverse[at, 0]) + dot(r, inverse[at, 1])))

    def downdate(d, k, j):
        block = (d, slice(k * TILE, (k + 1) * TILE), slice(j * TILE, (j + 1) * TILE))
        step = dot(pairs[d, k], high[block]) + dot(pairs[d, k], low[block])
        forward[d][j] = forward[d][j] - fold(step)

    def finish(d, k):
        c = coupling_ref[d, k * TILE : (k + 1) * TILE]
        total[d] = total[d] - fold(dot(pairs[d, k], c))

    for k in reversed(range(steps)):
        for d in everyone:
            retreat(d, k)
        for d in everyone:
            if d == 1 and k > 0:
                for e in everyone:
                    downdate(e, k, k - 1)
            if k + 1 < steps:
                finish(d, k + 1)
                for j in reversed(range(k)):
                    downdate(d, k + 1, j)
    for d in everyone:
        finish(d, 0)
    for s in range(slots):
        acc = jnp.zeros((cases, LANES), F32)
        for d in range(districts):
            tile, g = s // per, s % per
            within = ids_ref[d, s] % per
            piece = pltpu.roll(
                total[d][:, tile * LANES : (tile + 1) * LANES],
                ((within + per - g) % per) * BS,
                1,
            )
            acc = acc + jnp.where((group == within) & (s < live_ref[d]), piece, 0.0)
        out_ref[s] = acc


def apply(ids, live, gathered, coupling, factor, boundary):
    districts, size, faces = coupling.shape
    count = districts * (size // TILE)
    scalar = pl.BlockSpec(memory_space=pltpu.SMEM)
    whole = pl.BlockSpec(memory_space=pltpu.VMEM)
    return pl.pallas_call(
        apply_kernel,
        out_shape=jax.ShapeDtypeStruct(gathered.shape, F32),
        in_specs=[scalar, scalar] + [whole] * 4,
        out_specs=whole,
        scratch_shapes=[
            pltpu.VMEM((count * 2, LANES, LANES), F32),
            pltpu.VMEM((count, 2, TILE, TILE), BF),
            pltpu.VMEM((districts, size, size - TILE), BF),
            pltpu.VMEM((districts, size, size - TILE), BF),
        ],
        compiler_params=pltpu.CompilerParams(vmem_limit_bytes=28 << 20),
        cost_estimate=pl.CostEstimate(
            flops=10 * 10**9, bytes_accessed=24 << 20, transcendentals=0
        ),
        name="apply",
    )(ids, live, gathered, coupling, factor, boundary)


def pack_kernel(loads_ref, out_ref):
    loads = loads_ref[...]
    for p in range(out_ref.shape[0]):
        out_ref[p] = loads


def pack(loads, copies):
    whole = pl.BlockSpec(memory_space=pltpu.VMEM)
    return pl.pallas_call(
        pack_kernel,
        out_shape=jax.ShapeDtypeStruct((copies,) + loads.shape, F32),
        in_specs=[whole],
        out_specs=whole,
        compiler_params=pltpu.CompilerParams(vmem_limit_bytes=2 << 20),
        cost_estimate=pl.CostEstimate(
            flops=30 * 10**9, bytes_accessed=1 << 20, transcendentals=0
        ),
        name="pack",
    )(loads)


def body(factor, coupling, boundary, loads, block_ids, live_counts):
    gathered = lax.all_to_all(pack(loads, lax.axis_size("col")), "col", 0, 0)
    back = apply(block_ids, live_counts, gathered, coupling, factor, boundary)
    return jnp.sum(lax.all_to_all(back, "col", 0, 0), axis=0)


def solution(mesh):
    placed = (
        P(("row", "col"), None, None),
        P(("row", "col"), None, None),
        P(("row", "col"), None, None),
        P(None, ("row", "col")),
        P(("row", "col"), None),
        P(("row", "col")),
    )
    return jax.shard_map(
        body, mesh=mesh, in_specs=placed, out_specs=P(None, ("row", "col")), check_vma=False
    )
```

```python
import jax
import jax.numpy as jnp
from jax import lax
from jax.experimental import pallas as pl
from jax.experimental.pallas import tpu as pltpu
from jax.sharding import PartitionSpec as P

BS = 32
TILE = 256
HALF = TILE // 2
BASE = 16
BATCH = 12
LANES = 128
BF = jnp.bfloat16
F32 = jnp.float32


def split(a):
    high = a.astype(BF)
    return high, (a - high.astype(F32)).astype(BF)


def dot(a, b):
    return jnp.dot(a, b, preferred_element_type=F32)


def dot_t(a, b):
    return lax.dot_general(a, b, (((1,), (1,)), ((), ())), preferred_element_type=F32)


def dot3(a, b):
    both = dot(jnp.concatenate([a[0], a[1]], axis=1), jnp.concatenate([b[0], b[0]], axis=0))
    return both + dot(a[0], b[1])


def base_inverses(tiles):
    lane = lax.broadcasted_iota(jnp.int32, (BASE, LANES), 1)
    row = lax.broadcasted_iota(jnp.int32, (BASE, LANES), 0)
    group, column = lane // BASE, lane % BASE
    units, recips, states = [], [], []
    for tile in tiles:
        packed = tile[:BASE]
        for b in range(1, LANES // BASE):
            packed = jnp.where(group == b, tile[b * BASE : (b + 1) * BASE], packed)
        diagonal = jnp.sum(jnp.where(row == column, packed, 0.0), axis=0, keepdims=True)
        recip = 1.0 / diagonal
        recips.append(recip)
        units.append(jnp.where(row > column, packed * recip, 0.0))
        acc = jnp.where(row == column, 1.0, 0.0).astype(F32)
        states.append([acc[8 * g : 8 * g + 8] for g in range(BASE // 8)])
    for j in range(BASE - 1):
        yield
        index = group[:8] * BASE + j
        for unit, parts in zip(units, states):
            pivot = parts[j // 8][j % 8 : j % 8 + 1]
            for g in range((j + 1) // 8, BASE // 8):
                factor = jnp.take_along_axis(unit[8 * g : 8 * g + 8], index, axis=1)
                parts[g] = parts[g] - factor * pivot
    results = []
    for recip, parts in zip(recips, states):
        scale = jnp.take_along_axis(
            jnp.broadcast_to(recip, (BASE, LANES)), group * BASE + row, axis=1
        )
        results.append(jnp.concatenate(parts, axis=0) * scale)
    return results


def together(*tasks):
    tasks = [list(task) for task in tasks]
    while tasks:
        for task in list(tasks):
            for _ in range(task[1]):
                if next(task[0], tasks) is tasks:
                    tasks.remove(task)
                    break


def doubled(tiles, packed, width):
    group = lax.broadcasted_iota(jnp.int32, (width, LANES), 1) // width
    even = group % 2 == 0
    count = LANES // width
    products = []
    for tile, x in zip(tiles, packed):
        below = jnp.where(group == 0, tile[width : 2 * width], 0.0)
        for b in range(2, count, 2):
            below = jnp.where(group == b, tile[(b + 1) * width : (b + 2) * width], below)
        below = jnp.concatenate(split(below), axis=0)
        spread = [
            jnp.where(group == b, half, jnp.zeros_like(half))
            for half in split(x)
            for b in range(count)
        ]
        product = dot(jnp.concatenate([below, below], axis=1), jnp.concatenate(spread, axis=0))
        products.append(product[:width] + product[width:])
    yield
    results = []
    for x, product in zip(packed, products):
        odd = jnp.concatenate(split(jnp.where(even, 0.0, x)), axis=0)
        spread = []
        for half in split(product):
            zero = jnp.zeros_like(half)
            for b in range(0, count, 2):
                spread += [zero, jnp.where(group == b, half, zero)]
        product = dot(jnp.concatenate([odd, odd], axis=1), jnp.concatenate(spread, axis=0))
        corner = product[:width] + product[width:]
        results.append(
            jnp.concatenate([jnp.where(even, x, 0.0), jnp.where(even, -corner, x)], axis=0)
        )
    return results


def apply_kernel(
    ids_ref,
    live_ref,
    gathered_ref,
    coupling_ref,
    factor_ref,
    boundary_ref,
    out_ref,
    inv,
    inverse,
    high,
    low,
):
    slots, cases, _ = gathered_ref.shape
    districts, size, faces = coupling_ref.shape
    steps = size // TILE
    per = LANES // BS
    everyone = range(districts)

    blocks = [(d, k) for k in range(steps) for d in everyone]

    def tile_at(d, k, t, u):
        top, left = k * TILE + t * HALF, k * TILE + u * HALF
        return factor_ref[d, pl.ds(top, HALF), pl.ds(left, HALF)]

    def invert(batch):
        diagonal = [tile_at(d, k, t, t) for d, k in batch for t in range(2)]
        packed = yield from base_inverses(diagonal)
        width = BASE
        while width < HALF:
            yield
            packed = yield from doubled(diagonal, packed, width)
            width *= 2
        pairs = [(split(packed[2 * i]), split(packed[2 * i + 1])) for i in range(len(batch))]
        yield
        lefts = [dot3(split(tile_at(*at, 1, 0)), top) for at, (top, _) in zip(batch, pairs)]
        yield
        lefts = [split(-dot3(bottom, split(x))) for x, (_, bottom) in zip(lefts, pairs)]
        yield
        zero = jnp.zeros((HALF, HALF), BF)
        for (d, k), (top, bottom), left in zip(batch, pairs, lefts):
            at = d * steps + k
            for i in range(2):
                inverse[at, i, :HALF, :HALF] = top[i]
                inverse[at, i, :HALF, HALF:] = zero
                inverse[at, i, HALF:, :HALF] = left[i]
                inverse[at, i, HALF:, HALF:] = bottom[i]

    group = lax.broadcasted_iota(jnp.int32, (cases, LANES), 1) // BS

    def stack(a):
        return jnp.concatenate(split(a), axis=0)

    def fold(a):
        return a[:cases] + a[cases:]

    masked = []
    total, rest = [[] for _ in everyone], [[] for _ in everyone]
    def gather():
        for d in everyone:
            columns = []
            for tile in range(slots // per):
                acc = jnp.zeros((cases, LANES), F32)
                for g in range(per):
                    s = tile * per + g
                    within = ids_ref[d, s] % per
                    piece = pltpu.roll(gathered_ref[s], ((g + per - within) % per) * BS, 1)
                    acc = jnp.where((group == g) & (s < live_ref[d]), piece, acc)
                columns.append(acc)
            masked.append(stack(jnp.concatenate(columns, axis=1)))
        for k in range(steps):
            for d in everyone:
                yield
                right = dot_t(masked[d], coupling_ref[d, k * TILE : (k + 1) * TILE])
                rest[d].append(fold(right))

    def direct():
        for part in range(faces // LANES):
            for d in everyone:
                yield
                rows = slice(part * LANES, (part + 1) * LANES)
                parts = split(boundary_ref[d, rows])
                image = dot_t(masked[d], parts[0]) + dot_t(masked[d], parts[1])
                total[d].append(fold(image))

    forward = [[None] * steps for _ in everyone]
    pairs = {}

    def advance(d, k):
        at = d * steps + k
        r = stack(rest[d][k])
        forward[d][k] = fold(dot_t(r, inverse[at, 0]) + dot_t(r, inverse[at, 1]))
        pairs[d, k] = stack(forward[d][k])

    def update(d, k, j):
        block = (d, slice(j * TILE, (j + 1) * TILE), slice(k * TILE, (k + 1) * TILE))
        parts = split(factor_ref[block])
        high[block], low[block] = parts
        turned = split(factor_ref[block].T)
        step = dot(pairs[d, k], turned[0]) + dot(pairs[d, k], turned[1])
        rest[d][j] = rest[d][j] - fold(step)

    def solve(first, last):
        for k in range(first, last):
            for d in everyone:
                advance(d, k)
                yield
            for d in everyone:
                if d == 1 and k + 1 < steps:
                    for e in everyone:
                        update(e, k, k + 1)
                        yield
                if k > 0:
                    for j in range(k + 1, steps):
                        update(d, k - 1, j)
                        yield

    half = len(blocks) // 3
    together((invert(blocks[:half]), 1), (gather(), 1))
    together((invert(blocks[half:]), 1), (solve(0, 2), 1))
    def retreat(d, k):
        at = d * steps + k
        r = stack(forward[d][k])
        pairs[d, k] = stack(fold(dot(r, inverse[at, 0]) + dot(r, inverse[at, 1])))

    def downdate(d, k, j):
        block = (d, slice(k * TILE, (k + 1) * TILE), slice(j * TILE, (j + 1) * TILE))
        step = dot(pairs[d, k], high[block]) + dot(pairs[d, k], low[block])
        forward[d][j] = forward[d][j] - fold(step)

    def finish(d, k):
        c = coupling_ref[d, k * TILE : (k + 1) * TILE]
        image = fold(dot(pairs[d, k], c))
        minus[d] = image if minus[d] is None else minus[d] + image

    minus = [None] * districts

    def solve_back():
        for k in reversed(range(steps)):
            for d in everyone:
                retreat(d, k)
                yield
            for d in everyone:
                if d == 1 and k > 0:
                    for e in everyone:
                        downdate(e, k, k - 1)
                        yield
                if k + 1 < steps:
                    finish(d, k + 1)
                    yield
                    for j in reversed(range(k)):
                        downdate(d, k + 1, j)
                        yield
        for d in everyone:
            finish(d, 0)
            yield

    def both():
        yield from solve(steps - 2, steps)
        yield from solve_back()

    together((solve(2, steps - 2), 1))
    together((both(), 1), (direct(), 1))
    total = [jnp.concatenate(halves, axis=1) - m for halves, m in zip(total, minus)]
    for s in range(slots):
        acc = jnp.zeros((cases, LANES), F32)
        for d in range(districts):
            tile, g = s // per, s % per
            within = ids_ref[d, s] % per
            piece = pltpu.roll(
                total[d][:, tile * LANES : (tile + 1) * LANES],
                ((within + per - g) % per) * BS,
                1,
            )
            acc = acc + jnp.where((group == within) & (s < live_ref[d]), piece, 0.0)
        out_ref[s] = acc


def apply(ids, live, gathered, coupling, factor, boundary):
    districts, size, faces = coupling.shape
    count = districts * (size // TILE)
    scalar = pl.BlockSpec(memory_space=pltpu.SMEM)
    whole = pl.BlockSpec(memory_space=pltpu.VMEM)
    return pl.pallas_call(
        apply_kernel,
        out_shape=jax.ShapeDtypeStruct(gathered.shape, F32),
        in_specs=[scalar, scalar] + [whole] * 4,
        out_specs=whole,
        scratch_shapes=[
            pltpu.VMEM((count * 2, LANES, LANES), F32),
            pltpu.VMEM((count, 2, TILE, TILE), BF),
            pltpu.VMEM((districts, size, size - TILE), BF),
            pltpu.VMEM((districts, size, size - TILE), BF),
        ],
        compiler_params=pltpu.CompilerParams(vmem_limit_bytes=28 << 20),
        cost_estimate=pl.CostEstimate(
            flops=10 * 10**9, bytes_accessed=24 << 20, transcendentals=0
        ),
        name="apply",
    )(ids, live, gathered, coupling, factor, boundary)


def pack_kernel(loads_ref, out_ref):
    loads = loads_ref[...]
    for p in range(out_ref.shape[0]):
        out_ref[p] = loads


def pack(loads, copies):
    whole = pl.BlockSpec(memory_space=pltpu.VMEM)
    return pl.pallas_call(
        pack_kernel,
        out_shape=jax.ShapeDtypeStruct((copies,) + loads.shape, F32),
        in_specs=[whole],
        out_specs=whole,
        compiler_params=pltpu.CompilerParams(vmem_limit_bytes=2 << 20),
        cost_estimate=pl.CostEstimate(
            flops=30 * 10**9, bytes_accessed=1 << 20, transcendentals=0
        ),
        name="pack",
    )(loads)


def body(factor, coupling, boundary, loads, block_ids, live_counts):
    gathered = lax.all_to_all(pack(loads, lax.axis_size("col")), "col", 0, 0)
    back = apply(block_ids, live_counts, gathered, coupling, factor, boundary)
    return jnp.sum(lax.all_to_all(back, "col", 0, 0), axis=0)


def solution(mesh):
    placed = (
        P(("row", "col"), None, None),
        P(("row", "col"), None, None),
        P(("row", "col"), None, None),
        P(None, ("row", "col")),
        P(("row", "col"), None),
        P(("row", "col")),
    )
    return jax.shard_map(
        body, mesh=mesh, in_specs=placed, out_specs=P(None, ("row", "col")), check_vma=False
    )
```
